32 devices in a mesh: tile: 8 (over z, y), code: 4 (over x, core).
Axes of the slice: x: 2, y: 2, z: 4, core: 2. Of those that a mesh axis runs over, the one named last changes fastest.
Arguments:
- features: bfloat16 [8, 4, 1, 16, 32, 512], P('tile', 'code'), may hold values from -6 to 6
- w_first: bfloat16 [3, 3, 512, 512], replicated, may hold values from -0.09375 to 0.09375
- b_first: float32 [512], replicated, may hold values from -3 to 3
- w_latent: bfloat16 [3, 3, 512, 256], replicated, may hold values from -0.09375 to 0.09375
- b_latent: float32 [256], replicated, may hold values from -3 to 3
- codebook: bfloat16 [65536, 256], P(('tile', 'code')), may hold values from -6 to 6
- upstream: bfloat16 [8, 4, 1, 16, 32, 256], P('tile', 'code'), may hold values from -6 to 6
- owner: int32 [8, 4, 512, 1], P('tile', 'code'), may hold values from 0 to 31; in each aligned block of 512 rows (0 to 511, 512 to 1023, ..., all dimensions but the last counted through in order) at most 32 rows name the same one
- local_code: int32 [8, 4, 512], P('tile', 'code'), may hold values from 0 to 2047
Outputs:
- grad_latent: bfloat16 [8, 4, 1, 16, 32, 256], P('tile', 'code')
- row_loss: float32 [1, 128], P(None, 'tile')
- code_sums: float32 [65536, 256], P(('tile', 'code'))
- code_counts: float32 [65536], P(('tile', 'code'))
The draws below stay inside these ranges and needn't reach their ends.
Inputs may be any that keep to these rules, and one draw needn't show every extreme that they name: Among the tokens of one tile, at most 32 name the same owner, and exactly 32 do for some owner.
All inputs are finite; a program needn't handle non-finite values.
Results may differ from the reference program's by a relative error of at most 0.0025.
Values may be sent and summed in bfloat16 or wider, within the bound.
A program may use at most 64 MiB of HBM per device.

```python
import math
import jax
import jax.numpy as jnp
import numpy as np
from jax import lax

C = 512
L = 256
CODES_DEV = 2048
F = 1
RH = 16
RW = 32
GT = 8
GC = 4
W = 128
TOK_DEV = 512
CAP = 32
K = 65536
DEVICES = 32


def with_ends(array, stream_key, smallest, high):
    longest = array.shape.index(max(array.shape))
    spots = []
    for shift in (0, 1):
        where = [jax.random.randint(jax.random.fold_in(stream_key, axis), (), 0, length) for axis, length in enumerate(array.shape)]
        where[longest] = (where[longest] + shift) % array.shape[longest]
        spots.append(tuple(where))
    return array.at[spots[0]].set(smallest).at[spots[1]].set(high)


def steps_of(rng, shape, cuts, least, top_value):
    factor_of = 1.0
    for position, blocks in cuts:
        draws = jax.random.uniform(jax.random.fold_in(jax.random.fold_in(rng, 6), position), (blocks,), jnp.float32, least / len(cuts), top_value / len(cuts))
        factor_of = factor_of * jnp.repeat(jnp.exp(draws), shape[position] // blocks).reshape((-1,) + (1,) * (len(shape) - 1 - position))
    return factor_of


def rank_table(amount, slope):
    loads = [(1 << 20) // math.isqrt(rank ** slope) + 1 for rank in range(1, amount + 1)]
    scale = 1 + sum(loads) // (1 << 30)
    return np.cumsum(np.array([max(1, weight // scale) for weight in loads]))


def ranked_ids(stream_key, extent, amount, lean):
    table = rank_table(amount, lean)
    ticket = jax.random.randint(jax.random.fold_in(stream_key, 1), extent, 0, int(table[amount - 1]))
    grade = jnp.searchsorted(jnp.asarray(table, jnp.int32), ticket, side="right")
    return jax.random.permutation(jax.random.fold_in(stream_key, 2), amount)[grade].astype(jnp.int32)


def deal_out(rng, own, number, rows, count, top, reach, lean):
    ranking = jax.random.permutation(rng, count)
    heavy_load, usual = load_shares(count, rows * top, reach, lean, True), load_shares(count, rows * top, reach, lean, False)
    places = jnp.arange(count)

    def named(tallies, turn):
        used = int((tallies > 0).sum())
        fixed = max(1, used // 4)
        moved = fixed + (places - fixed + turn * (used - fixed)) % max(1, count - fixed)
        return jnp.zeros((count,), jnp.int32).at[ranking[jnp.where(places < fixed, places, moved)]].set(jnp.asarray(tallies, jnp.int32))

    tallies = jnp.where(number % 4 == 0, named(heavy_load, number // 4), named(usual, number - number // 4 - 1))
    mixed = jax.random.permutation(jax.random.fold_in(own, 3), count)
    giver, taker = mixed[0:count // 2 * 2:2], mixed[1:count // 2 * 2:2]
    margin = jnp.minimum(tallies[giver] - 1, reach - tallies[taker]) // 2
    margin = jnp.where((giver == ranking[0]) | (taker == ranking[0]) | (tallies[taker] == 0), 0, jnp.maximum(margin, 0))
    moved = jax.random.randint(jax.random.fold_in(own, 4), (count // 2,), 0, 1 << 20) % (margin + 1)
    tallies = tallies.at[giver].add(-moved).at[taker].add(moved)
    items = jnp.searchsorted(jnp.cumsum(tallies), jnp.arange(rows * top), side="right").astype(jnp.int32)
    table = items.reshape(top, rows).T
    table = table[jax.random.permutation(jax.random.fold_in(own, 1), rows)]
    turn = jax.random.randint(jax.random.fold_in(own, 2), (rows, 1), 0, top)
    return jnp.take_along_axis(table, (jnp.arange(top)[None, :] + turn) % top, axis=1)


def load_shares(count, total, bound, skew, full):
    weights = [(1 << 20) // math.isqrt(rank ** skew) + 1 for rank in range(1, count + 1)]
    largest = bound if full else min(bound, max(-(-total // count), total * weights[0] // sum(weights)))
    least = 1 if total - largest >= count - 1 else 0
    given, spare = [largest] + [least] * (count - 1), total - largest - least * (count - 1)
    while spare > 0:
        movable = [i for i in range(1, count) if given[i] < largest] or [i for i in range(1, count) if given[i] < bound]
        mass, left = sum([weights[i] for i in movable]), spare
        for i in movable:
            more = min(bound - given[i], max(1, left * weights[i] // mass), spare)
            given[i] = given[i] + more
            spare = spare - more
    return np.array(given)


def bell_draw(key, extent, scale, bound, cuts=(), kind=jnp.bfloat16):
    gain = steps_of(key, extent, cuts, -0.22, 0.18) if cuts else 1.0
    array = jax.random.normal(key, extent, jnp.float32) * scale * gain
    return jnp.minimum(jnp.maximum(array, -bound), bound).astype(kind)


def setup_inputs(seed: int = 0) -> dict:
    arg_keys = jax.random.split(jax.random.key(seed), 10)
    features = bell_draw(arg_keys[0], (GT, GC, F, RH, RW, C), 1.0, 6.0, ((0, 8), (1, 4)))
    w_first = bell_draw(arg_keys[1], (3, 3, C, C), (9 * C) ** -0.5, 0.09375)
    b_first = bell_draw(arg_keys[2], (C,), 0.5, 3.0, (), jnp.float32)
    w_latent = bell_draw(arg_keys[3], (3, 3, C, L), (9 * C) ** -0.5, 0.09375)
    b_latent = bell_draw(arg_keys[4], (L,), 0.5, 3.0, (), jnp.float32)
    codebook = bell_draw(arg_keys[5], (K, L), 1.0, 6.0, ((0, 32),))
    upstream = bell_draw(arg_keys[6], (GT, GC, F, RH, RW, L), 1.0, 6.0, ((0, 8), (1, 4)))
    owner_keys = jax.random.split(jax.random.fold_in(arg_keys[7], 1), GT * GC * TOK_DEV // TOK_DEV)
    owner_turns = jax.random.permutation(jax.random.fold_in(arg_keys[7], 3), GT * GC * TOK_DEV // TOK_DEV)
    owner = jax.vmap(lambda own, number: deal_out(jax.random.fold_in(arg_keys[7], 2), own, number, TOK_DEV, DEVICES, 1, CAP, 2))(owner_keys, owner_turns).reshape((GT, GC, TOK_DEV, 1))
    local_code = with_ends(ranked_ids(arg_keys[8], (GT, GC, TOK_DEV), CODES_DEV, 2), jax.random.fold_in(arg_keys[8], 3), 0, CODES_DEV - 1).astype(jnp.int32)
    return {"features": features, "w_first": w_first, "b_first": b_first, "w_latent": w_latent, "b_latent": b_latent, "codebook": codebook, "upstream": upstream, "owner": owner, "local_code": local_code}


BETA = 0.25


def to_grid(tiles):
    tile_rows, tile_cols, frame_count, row_count, col_count, width = tiles.shape
    moved = jnp.transpose(tiles, (2, 0, 3, 1, 4, 5))
    return moved.reshape(frame_count, tile_rows * row_count, tile_cols * col_count, width)


def to_tiles(grid, tile_rows, tile_cols):
    frame_count, height, breadth, width = grid.shape
    row_count = height // tile_rows
    col_count = breadth // tile_cols
    split = grid.reshape(frame_count, tile_rows, row_count, tile_cols, col_count, width)
    return jnp.transpose(split, (1, 3, 0, 2, 4, 5))


def convolve(field, weight):
    return lax.conv_general_dilated(field, weight, (1, 1), "SAME", dimension_numbers=("NHWC", "HWIO", "NHWC"), preferred_element_type=jnp.float32)


def reference(features, w_first, b_first, w_latent, b_latent, codebook, upstream, owner, local_code):
    grid = to_grid(features)
    hidden = jax.nn.silu(convolve(grid, w_first) + b_first).astype(jnp.bfloat16)
    latent = convolve(hidden, w_latent) + b_latent
    latent_tiles = to_tiles(latent, GT, GC)
    flat_latent = latent_tiles.reshape(GT, GC, TOK_DEV, L)
    index = owner[..., 0] * CODES_DEV + local_code
    chosen = codebook[index].astype(jnp.float32)
    differ = flat_latent - chosen
    grad_flat = upstream.reshape(GT, GC, TOK_DEV, L).astype(jnp.float32) + 2.0 * BETA * differ
    grad_latent = grad_flat.astype(jnp.bfloat16).reshape(upstream.shape)
    cell_error = jnp.sum(differ * differ, axis=-1).reshape(GT, GC, F, RH, RW, 1)
    error_grid = to_grid(cell_error)[..., 0]
    row_loss = BETA * jnp.sum(error_grid, axis=2) / (W * L)
    flat_index = index.reshape(-1)
    code_sums = jnp.zeros((K, L), jnp.float32).at[flat_index].add(flat_latent.reshape(-1, L))
    code_counts = jnp.zeros((K,), jnp.float32).at[flat_index].add(jnp.ones(flat_index.shape, jnp.float32))
    return grad_latent, row_loss, code_sums, code_counts
```

```python
import functools

import jax
import jax.numpy as jnp
from jax import lax
from jax.experimental import pallas as pl
from jax.experimental.pallas import tpu as pltpu
from jax.sharding import PartitionSpec as P

BETA = 0.25
BF, F32, I32 = jnp.bfloat16, jnp.float32, jnp.int32
MESH = pl.DeviceIdType.MESH
LANES = 128


def iota(shape, dim):
    return lax.broadcasted_iota(I32, shape, dim)


def dot(a, b):
    return jnp.dot(a, b, preferred_element_type=F32)


def body(
    tiles, cols_of, rows, cols, cap,
    x_ref, w1_hbm, b1_ref, w2_hbm, b2_ref, book_hbm, up_hbm, own_ref, loc_ref,
    grad_ref, loss_ref, sums_ref, counts_ref,
    w1, w2, book, up, pack, top, bot, side, corner, colbuf, im1, hid, im2,
    req_out, req_in, onehot, onehot_t, pick, pick_t, ans, ret, par, arr, loss_out, loss_in,
    local_sem, halo_send, halo_recv, send_sem, recv_sem,
):
    n = tiles * cols_of
    tok = rows * cols
    width = x_ref.shape[1]
    codes = book.shape[0]
    slots = n * cap
    groups = slots // LANES
    per = LANES // cap
    shift = cols.bit_length() - 1
    a, b = lax.axis_index("tile"), lax.axis_index("code")
    me = a * cols_of + b

    loads = []
    for i, (src, dst) in enumerate(((book_hbm, book), (w1_hbm, w1), (w2_hbm, w2), (up_hbm, up))):
        copy = pltpu.make_async_copy(src, dst, local_sem.at[i])
        copy.start()
        loads.append(copy)

    def place_of(i):
        d = lax.rem(me + i, n)
        return d, (d // cols_of, lax.rem(d, cols_of))

    barrier = pltpu.get_barrier_semaphore()

    def greet(i, _):
        pl.semaphore_signal(barrier, inc=1, device_id=place_of(i)[1], device_id_type=MESH)
        return 0

    lax.fori_loop(1, n, greet, 0)

    o = iota((128, tok), 0)
    t = iota((128, tok), 1)
    col_row, col_col = o & 15, ((o >> 4) & 1) + (o >> 5) * (cols - 2)
    k, q = o & 15, (o >> 4) & 3
    cor_row = (k >> 1) + (q >> 1) * (rows - 2)
    cor_col = (k & 1) + (q & 1) * (cols - 2)
    from_col = (o < 64) & (t == col_row * cols + col_col)
    from_cor = (o >= 64) & (k < 4) & (t == cor_row * cols + cor_col)
    pack[...] = dot(jnp.where(from_col | from_cor, 1.0, 0.0).astype(BF), x_ref[...]).astype(BF)

    own = own_ref[...]
    loc = loc_ref[...]
    member = jnp.where(iota((n, tok), 0) == own, 1.0, 0.0)
    before = jnp.where(iota((tok, tok), 0) < iota((tok, tok), 1), 1.0, 0.0).astype(BF)
    earlier = dot(member.astype(BF), before)
    rank = jnp.sum(member * earlier, axis=0, keepdims=True)
    place = own.astype(F32) * cap + rank
    r8 = iota((8, tok), 0)
    stack = jnp.where(r8 == 0, rank, jnp.where(r8 == 1, loc.astype(F32), place))
    columns = jnp.transpose(stack)
    rank_c, loc_c, place_c = columns[:, 0:1], columns[:, 1:2], columns[:, 2:3]
    high = jnp.floor(loc_c * (1.0 / 64.0))
    low = loc_c - high * 64.0 + 1.0
    lane = iota((tok, LANES), 1).astype(F32)
    seat = lane == rank_c + (lax.rem(me, per) * cap).astype(F32)
    asked_high = dot(member.astype(BF), jnp.where(seat, high, 0.0).astype(BF))
    asked_low = dot(member.astype(BF), jnp.where(seat, low, 0.0).astype(BF))
    wanted = asked_high * 64.0 + asked_low
    for d in range(n):
        req_out[d] = jnp.broadcast_to(wanted[d : d + 1, :], (8, LANES))
    req_in[me] = req_out[me]

    up_ok, down_ok = a > 0, a < tiles - 1
    left_ok, right_ok = b > 0, b < cols_of - 1
    hops = (
        (up_ok, -1, 0), (down_ok, 1, 0), (left_ok, 0, -1), (right_ok, 0, 1),
        (up_ok & left_ok, -1, -1), (up_ok & right_ok, -1, 1),
        (down_ok & left_ok, 1, -1), (down_ok & right_ok, 1, 1),
    )
    edge = 2 * cols
    outgoing = (
        x_ref.at[pl.ds(0, edge)], x_ref.at[pl.ds(tok - edge, edge)],
        pack.at[pl.ds(0, 32)], pack.at[pl.ds(32, 32)],
        pack.at[pl.ds(64, 16)], pack.at[pl.ds(80, 16)],
        pack.at[pl.ds(96, 16)], pack.at[pl.ds(112, 16)],
    )
    landing = (top, bot, side.at[0], side.at[1], corner.at[0], corner.at[1], corner.at[2], corner.at[3])
    opposite = (1, 0, 3, 2, 7, 6, 5, 4)

    def halo(i):
        _, da, db = hops[i]
        return pltpu.make_async_remote_copy(
            src_ref=outgoing[i], dst_ref=landing[opposite[i]],
            send_sem=halo_send.at[i], recv_sem=halo_recv.at[opposite[i]],
            device_id=(a + da, b + db), device_id_type=MESH,
        )

    def arrival(i):
        return pltpu.make_async_copy(landing[i], landing[i], halo_recv.at[i])

    pl.semaphore_wait(barrier, n - 1)

    def send_all(src, dst, phase, rows_each):
        def step(i, _):
            d, where = place_of(i)
            if rows_each is None:
                s, r = src.at[d], dst.at[me]
            else:
                s = src.at[pl.ds(pl.multiple_of(d * rows_each, rows_each), rows_each)]
                r = dst.at[pl.ds(pl.multiple_of(me * rows_each, rows_each), rows_each)]
            pltpu.make_async_remote_copy(
                src_ref=s, dst_ref=r, send_sem=send_sem.at[phase], recv_sem=recv_sem.at[phase],
                device_id=where, device_id_type=MESH,
            ).start()
            return 0

        lax.fori_loop(1, n, step, 0)

    def wait_all(buf, sem, rows_each):
        part = buf.at[pl.ds(0, (n - 1) * (1 if rows_each is None else rows_each))]
        pltpu.make_async_copy(part, part, sem).wait()

    send_all(req_out, req_in, 0, None)
    for i in range(8):
        pl.when(hops[i][0])(lambda i=i: halo(i).start())

        @pl.when(jnp.logical_not(hops[i][0]))
        def _(i=i):
            landing[i][...] = jnp.zeros(landing[i].shape, BF)

    pick[...] = jnp.where(iota((slots, tok), 0).astype(F32) == place, 1.0, 0.0).astype(BF)
    pick_t[...] = jnp.where(iota((tok, slots), 1).astype(F32) == place_c, 1.0, 0.0).astype(BF)

    loads[0].wait()
    wait_all(req_in, recv_sem.at[0], None)
    sub8 = iota((8, LANES), 0)
    asked = []
    for g in range(groups):
        total = req_in[g * per]
        for j in range(1, per):
            total = total + req_in[g * per + j]
        asked.append(total)
    for g8 in range(groups // 8):
        table = jnp.zeros((8, LANES), F32)
        for g in range(8):
            table = jnp.where(sub8 == g, asked[g8 * 8 + g], table)
        table = jnp.transpose(table)
        for g in range(8):
            first = (g8 * 8 + g) * LANES
            hot = iota((LANES, codes), 1).astype(F32) + 1.0 == table[:, g : g + 1]
            onehot[pl.ds(first, LANES), :] = jnp.where(hot, 1.0, 0.0).astype(BF)
    ans[...] = dot(onehot[...], book[...]).astype(BF)
    mine = pl.ds(pl.multiple_of(me * cap, cap), cap)
    ret[mine, :] = ans[mine, :]
    send_all(ans, ret, 1, cap)

    for i in range(8):
        pl.when(hops[i][0])(lambda i=i: arrival(i).wait())
    for s in range(2):
        for c in range(2):
            slot = (0, 1, 4, 5)[s * 2 + c]
            colbuf[slot, 8:24, :] = side[s, c * 16 : c * 16 + 16, :].astype(F32)
        slot = 2 + s
        edge_col = s * (cols - 1)
        colbuf[slot, 8:24, :] = pack[s * 48 : s * 48 + 16, :].astype(F32)
        tf, bf_ = top[...].astype(F32), bot[...].astype(F32)
        for r in range(2):
            at = r * cols + edge_col
            colbuf[slot, 6 + r : 7 + r, :] = tf[at : at + 1, :]
            colbuf[slot, 24 + r : 25 + r, :] = bf_[at : at + 1, :]
    for q in range(4):
        piece = corner[q].astype(F32)
        for r in range(2):
            for c in range(2):
                slot = (0, 1, 4, 5)[(q % 2) * 2 + c]
                at = (6 if q < 2 else 24) + r
                colbuf[slot, at : at + 1, :] = piece[r * 2 + c : r * 2 + c + 1, :]
    for slot in range(6):
        colbuf[slot, 26:32, :] = jnp.zeros((6, width), F32)
    sub = iota((cols, width), 0)

    def spread(buf, count, r, three):
        for dx in range(3):
            for dy in range(3):
                if 0 <= r - dy < count:
                    buf[(r - dy) * cols : (r - dy + 1) * cols, (dy * 3 + dx) * width : (dy * 3 + dx + 1) * width] = three[dx]

    def shifted(row, before_col, after_col):
        left = jnp.where(sub == 0, before_col, pltpu.roll(row, 1, 0))
        right = jnp.where(sub == cols - 1, after_col, pltpu.roll(row, cols - 1, 0))
        return left.astype(BF), row.astype(BF), right.astype(BF)

    for r in range(rows + 4):
        if r < 2:
            row = top[r * cols : (r + 1) * cols, :]
        elif r < rows + 2:
            row = x_ref[(r - 2) * cols : (r - 1) * cols, :]
        else:
            row = bot[(r - rows - 2) * cols : (r - rows - 1) * cols, :]
        three = shifted(row.astype(F32), colbuf[1, 6 + r : 7 + r, :], colbuf[4, 6 + r : 7 + r, :])
        spread(im1, rows + 2, r, three)
    main = (rows + 2) * cols
    for dy in range(3):
        for dx in range(3):
            both = jnp.concatenate(
                [colbuf[dx, 6 + dy : 30 + dy, :], colbuf[3 + dx, 6 + dy : 30 + dy, :]], axis=0
            )
            im1[main : main + 48, (dy * 3 + dx) * width : (dy * 3 + dx + 1) * width] = both.astype(BF)
    loads[1].wait()
    value = dot(im1[...], w1[...]) + b1_ref[...]
    hid[...] = value / (1.0 + jnp.exp(-value))

    tall = [jnp.where(ok, 1.0, 0.0).astype(F32) for ok in (up_ok, down_ok, left_ok, right_ok)]
    for r in range(rows + 2):
        row = hid[r * cols : (r + 1) * cols, :]
        before_col = hid[main + r : main + r + 1, :] * tall[2]
        after_col = hid[main + 24 + r : main + 25 + r, :] * tall[3]
        if r in (0, rows + 1):
            f = tall[0 if r == 0 else 1]
            row, before_col, after_col = row * f, before_col * f, after_col * f
        spread(im2, rows, r, shifted(row, before_col, after_col))
    loads[2].wait()
    latent = dot(im2[...], w2[...]) + b2_ref[...]
    par[...] = dot(pick[...], latent.astype(BF)).astype(BF)
    arr[mine, :] = par[mine, :]
    send_all(par, arr, 2, cap)

    loads[3].wait()
    for g in range(groups):
        hot = (iota((codes, LANES), 0).astype(F32) + 1.0) == asked[g][0:1, :]
        onehot_t[:, g * LANES : (g + 1) * LANES] = jnp.where(hot, 1.0, 0.0).astype(BF)
    counts_ref[...] = dot(jnp.ones((8, slots), BF), onehot[...])[0:1, :]
    wait_all(ret, recv_sem.at[1], cap)
    chosen = dot(pick_t[...], ret[...])
    differ = latent - chosen
    grad_ref[...] = (up[...].astype(F32) + 2.0 * BETA * differ).astype(BF)
    square = differ * differ
    half = square[:, 0:LANES]
    for j in range(1, square.shape[1] // LANES):
        half = half + square[:, j * LANES : (j + 1) * LANES]
    part = jnp.sum(half.reshape(rows, cols, LANES), axis=1)
    loss_out[...] = part
    loss_in[b] = part

    def loss_copy(i):
        peer = lax.rem(b + i, cols_of)
        return pltpu.make_async_remote_copy(
            src_ref=loss_out, dst_ref=loss_in.at[b], send_sem=send_sem.at[3], recv_sem=recv_sem.at[3],
            device_id=(a, peer), device_id_type=MESH,
        )

    for i in range(1, cols_of):
        loss_copy(i).start()

    wait_all(arr, recv_sem.at[2], cap)
    sums_ref[...] = dot(onehot_t[...], arr[...])
    others = loss_in.at[pl.ds(0, cols_of - 1)]
    pltpu.make_async_copy(others, others, recv_sem.at[3]).wait()
    total = loss_in[0]
    for i in range(1, cols_of):
        total = total + loss_in[i]
    line = jnp.sum(jnp.transpose(total), axis=0, keepdims=True)
    loss_ref[...] = BETA * line / (cols * cols_of * square.shape[1])

    pltpu.make_async_copy(others, others, send_sem.at[3]).wait()
    wait_all(req_out, send_sem.at[0], None)
    wait_all(ans, send_sem.at[1], cap)
    wait_all(par, send_sem.at[2], cap)
    for i in range(8):
        pl.when(hops[i][0])(lambda i=i: halo(i).wait_send())


def shards(features, w_first, b_first, w_latent, b_latent, codebook, upstream, owner, local_code):
    tiles, cols_of = lax.axis_size("tile"), lax.axis_size("code")
    n = tiles * cols_of
    rows, cols, width = features.shape[3:]
    tok, latent = rows * cols, w_latent.shape[3]
    codes = codebook.shape[0]
    cap = max(16, 2 * tok // n)
    slots = n * cap
    deep = 9 * width
    vmem = pl.BlockSpec(memory_space=pltpu.VMEM)
    anyw = pl.BlockSpec(memory_space=pl.ANY)
    grad, loss, sums, counts = pl.pallas_call(
        functools.partial(body, tiles, cols_of, rows, cols, cap),
        out_shape=(
            jax.ShapeDtypeStruct((tok, latent), BF),
            jax.ShapeDtypeStruct((1, rows), F32),
            jax.ShapeDtypeStruct((codes, latent), F32),
            jax.ShapeDtypeStruct((1, codes), F32),
        ),
        in_specs=[vmem, anyw, vmem, anyw, vmem, anyw, anyw, vmem, vmem],
        out_specs=(vmem, vmem, vmem, vmem),
        scratch_shapes=[
            pltpu.VMEM((deep, width), BF),
            pltpu.VMEM((deep, latent), BF),
            pltpu.VMEM((codes, latent), BF),
            pltpu.VMEM((tok, latent), BF),
            pltpu.VMEM((128, width), BF),
            pltpu.VMEM((2 * cols, width), BF),
            pltpu.VMEM((2 * cols, width), BF),
            pltpu.VMEM((2, 32, width), BF),
            pltpu.VMEM((4, 16, width), BF),
            pltpu.VMEM((6, 32, width), F32),
            pltpu.VMEM(((rows + 2) * cols + 48, deep), BF),
            pltpu.VMEM(((rows + 2) * cols + 48, width), F32),
            pltpu.VMEM((tok, deep), BF),
            pltpu.VMEM((n, 8, LANES), F32),
            pltpu.VMEM((n, 8, LANES), F32),
            pltpu.VMEM((slots, codes), BF),
            pltpu.VMEM((codes, slots), BF),
            pltpu.VMEM((slots, tok), BF),
            pltpu.VMEM((tok, slots), BF),
            pltpu.VMEM((slots, latent), BF),
            pltpu.VMEM((slots, latent), BF),
            pltpu.VMEM((slots, latent), BF),
            pltpu.VMEM((slots, latent), BF),
            pltpu.VMEM((rows, LANES), F32),
            pltpu.VMEM((cols_of, rows, LANES), F32),
            pltpu.SemaphoreType.DMA((4,)),
            pltpu.SemaphoreType.DMA((8,)),
            pltpu.SemaphoreType.DMA((8,)),
            pltpu.SemaphoreType.DMA((4,)),
            pltpu.SemaphoreType.DMA((4,)),
        ],
        compiler_params=pltpu.CompilerParams(
            collective_id=0, has_side_effects=True, vmem_limit_bytes=60 * 1024 * 1024
        ),
        name="quantize",
    )(
        features.reshape(tok, width),
        w_first.reshape(deep, width),
        b_first.reshape(1, width),
        w_latent.reshape(deep, latent),
        b_latent.reshape(1, latent),
        codebook,
        upstream.reshape(tok, latent),
        owner.reshape(1, tok),
        local_code.reshape(1, tok),
    )
    return grad.reshape(upstream.shape), loss, sums, counts.reshape(codes)


def solution(mesh):
    in_specs = (
        P("tile", "code", None, None, None, None),
        P(),
        P(),
        P(),
        P(),
        P(("tile", "code"), None),
        P("tile", "code", None, None, None, None),
        P("tile", "code", None, None),
        P("tile", "code", None),
    )
    out_specs = (
        P("tile", "code", None, None, None, None),
        P(None, "tile"),
        P(("tile", "code"), None),
        P(("tile", "code")),
    )
    return jax.shard_map(shards, mesh=mesh, in_specs=in_specs, out_specs=out_specs, check_vma=False)
```

```python
import functools
import math

import jax
import jax.numpy as jnp
from jax import lax
from jax.experimental import pallas as pl
from jax.experimental.pallas import tpu as pltpu
from jax.sharding import PartitionSpec as P

BETA = 0.25
BF, F32, I32 = jnp.bfloat16, jnp.float32, jnp.int32
MESH = pl.DeviceIdType.MESH
LANES = 128


def iota(shape, dim):
    return lax.broadcasted_iota(I32, shape, dim)


def dot(a, b):
    return jnp.dot(a, b, preferred_element_type=F32)


def body(
    tiles, cols_of, rows, cols, cap,
    x_ref, w1_hbm, b1_ref, w2_hbm, b2_ref, book_hbm, up_hbm, own_ref, loc_ref,
    grad_ref, loss_ref, counts_ref, asked_ref, arr,
    w1, w2, book, up, pack, top, bot, side, corner, colbuf, im1, hid, im2,
    req_out, req_in, onehot, pick, pick_t, ans, ret, par, loss_out, loss_in,
    local_sem, halo_send, halo_recv, send_sem, recv_sem,
):
    n = tiles * cols_of
    tok = rows * cols
    width = x_ref.shape[1]
    codes = book.shape[0]
    slots = n * cap
    groups = slots // LANES
    per = LANES // cap
    hop = next(h for h in range(2 * n // 5, n) if math.gcd(h, n) == 1)
    a, b = lax.axis_index("tile"), lax.axis_index("code")
    me = a * cols_of + b

    loads = []
    for i, (src, dst) in enumerate(((book_hbm, book), (w1_hbm, w1), (w2_hbm, w2), (up_hbm, up))):
        copy = pltpu.make_async_copy(src, dst, local_sem.at[i])
        copy.start()
        loads.append(copy)

    def place_of(i):
        d = jnp.bitwise_xor(me, i)
        return d, (d // cols_of, lax.rem(d, cols_of))

    barrier = pltpu.get_barrier_semaphore()

    def greet(i, _):
        pl.semaphore_signal(barrier, inc=1, device_id=place_of(i)[1], device_id_type=MESH)
        return 0

    lax.fori_loop(1, n, greet, 0)

    o = iota((128, tok), 0)
    t = iota((128, tok), 1)
    col_row, col_col = o & 15, ((o >> 4) & 1) + (o >> 5) * (cols - 2)
    k, q = o & 15, (o >> 4) & 3
    cor_row = (k >> 1) + (q >> 1) * (rows - 2)
    cor_col = (k & 1) + (q & 1) * (cols - 2)
    from_col = (o < 64) & (t == col_row * cols + col_col)
    from_cor = (o >= 64) & (k < 4) & (t == cor_row * cols + cor_col)
    pack[...] = dot(jnp.where(from_col | from_cor, 1.0, 0.0).astype(BF), x_ref[...]).astype(BF)

    own = own_ref[...]
    loc = loc_ref[...]
    member = jnp.where(iota((n, tok), 0) == own, 1.0, 0.0)
    before = jnp.where(iota((tok, tok), 0) < iota((tok, tok), 1), 1.0, 0.0).astype(BF)
    earlier = dot(member.astype(BF), before)
    rank = jnp.sum(member * earlier, axis=0, keepdims=True)
    place = own.astype(F32) * cap + rank
    r8 = iota((8, tok), 0)
    stack = jnp.where(r8 == 0, rank, jnp.where(r8 == 1, loc.astype(F32), place))
    columns = jnp.transpose(stack)
    rank_c, loc_c, place_c = columns[:, 0:1], columns[:, 1:2], columns[:, 2:3]
    high = jnp.floor(loc_c * (1.0 / 64.0))
    low = loc_c - high * 64.0 + 1.0
    lane = iota((tok, LANES), 1).astype(F32)
    seat = lane == rank_c + (lax.rem(me, per) * cap).astype(F32)
    asked_high = dot(member.astype(BF), jnp.where(seat, high, 0.0).astype(BF))
    asked_low = dot(member.astype(BF), jnp.where(seat, low, 0.0).astype(BF))
    wanted = asked_high * 64.0 + asked_low
    for d in range(n):
        req_out[d] = jnp.broadcast_to(wanted[d : d + 1, :], (8, LANES))
    req_in[me] = req_out[me]

    up_ok, down_ok = a > 0, a < tiles - 1
    left_ok, right_ok = b > 0, b < cols_of - 1
    hops = (
        (up_ok, -1, 0), (down_ok, 1, 0), (left_ok, 0, -1), (right_ok, 0, 1),
        (up_ok & left_ok, -1, -1), (up_ok & right_ok, -1, 1),
        (down_ok & left_ok, 1, -1), (down_ok & right_ok, 1, 1),
    )
    edge = 2 * cols
    outgoing = (
        x_ref.at[pl.ds(0, edge)], x_ref.at[pl.ds(tok - edge, edge)],
        pack.at[pl.ds(0, 32)], pack.at[pl.ds(32, 32)],
        pack.at[pl.ds(64, 16)], pack.at[pl.ds(80, 16)],
        pack.at[pl.ds(96, 16)], pack.at[pl.ds(112, 16)],
    )
    landing = (top, bot, side.at[0], side.at[1], corner.at[0], corner.at[1], corner.at[2], corner.at[3])
    opposite = (1, 0, 3, 2, 7, 6, 5, 4)

    def halo(i):
        _, da, db = hops[i]
        return pltpu.make_async_remote_copy(
            src_ref=outgoing[i], dst_ref=landing[opposite[i]],
            send_sem=halo_send.at[i], recv_sem=halo_recv.at[opposite[i]],
            device_id=(a + da, b + db), device_id_type=MESH,
        )

    def arrival(i):
        return pltpu.make_async_copy(landing[i], landing[i], halo_recv.at[i])

    pl.semaphore_wait(barrier, n - 1)

    def send_all(src, dst, phase, rows_each):
        def step(i, _):
            d, where = place_of(i)
            if rows_each is None:
                s, r = src.at[d], dst.at[me]
            else:
                s = src.at[pl.ds(pl.multiple_of(d * rows_each, rows_each), rows_each)]
                r = dst.at[pl.ds(pl.multiple_of(me * rows_each, rows_each), rows_each)]
            pltpu.make_async_remote_copy(
                src_ref=s, dst_ref=r, send_sem=send_sem.at[phase], recv_sem=recv_sem.at[phase],
                device_id=where, device_id_type=MESH,
            ).start()
            return 0

        lax.fori_loop(1, n, step, 0)

    def wait_all(buf, sem, rows_each):
        part = buf.at[pl.ds(0, (n - 1) * (1 if rows_each is None else rows_each))]
        pltpu.make_async_copy(part, part, sem).wait()

    send_all(req_out, req_in, 0, None)
    for i in range(8):
        pl.when(hops[i][0])(lambda i=i: halo(i).start())

        @pl.when(jnp.logical_not(hops[i][0]))
        def _(i=i):
            landing[i][...] = jnp.zeros(landing[i].shape, BF)

    pick[...] = jnp.where(iota((slots, tok), 0).astype(F32) == place, 1.0, 0.0).astype(BF)
    pick_t[...] = jnp.where(iota((tok, slots), 1).astype(F32) == place_c, 1.0, 0.0).astype(BF)

    loads[0].wait()
    wait_all(req_in, recv_sem.at[0], None)
    own_group = me // per
    code_lane = iota((LANES, codes), 1).astype(F32) + 1.0

    def answer(g, _):
        group = jnp.bitwise_xor(own_group, groups - 1 - g)
        total = req_in[group * per]
        for j in range(1, per):
            total = total + req_in[group * per + j]
        asked_ref[group] = total
        here = pl.ds(pl.multiple_of(group * LANES, LANES), LANES)
        hot = jnp.where(code_lane == jnp.transpose(total)[:, 0:1], 1.0, 0.0).astype(BF)
        onehot[here, :] = hot
        ans[here, :] = dot(hot, book[...]).astype(BF)
        for j in range(per):
            d = group * per + j

            @pl.when(d != me)
            def _():
                pltpu.make_async_remote_copy(
                    src_ref=ans.at[pl.ds(pl.multiple_of(d * cap, cap), cap)],
                    dst_ref=ret.at[pl.ds(pl.multiple_of(me * cap, cap), cap)],
                    send_sem=send_sem.at[1], recv_sem=recv_sem.at[1],
                    device_id=(d // cols_of, lax.rem(d, cols_of)), device_id_type=MESH,
                ).start()
        return 0

    lax.fori_loop(0, groups, answer, 0)
    mine = pl.ds(pl.multiple_of(me * cap, cap), cap)
    ret[mine, :] = ans[mine, :]

    for i in range(8):
        pl.when(hops[i][0])(lambda i=i: arrival(i).wait())
    for s in range(2):
        for c in range(2):
            slot = (0, 1, 4, 5)[s * 2 + c]
            colbuf[slot, 8:24, :] = side[s, c * 16 : c * 16 + 16, :].astype(F32)
        slot = 2 + s
        edge_col = s * (cols - 1)
        colbuf[slot, 8:24, :] = pack[s * 48 : s * 48 + 16, :].astype(F32)
        tf, bf_ = top[...].astype(F32), bot[...].astype(F32)
        for r in range(2):
            at = r * cols + edge_col
            colbuf[slot, 6 + r : 7 + r, :] = tf[at : at + 1, :]
            colbuf[slot, 24 + r : 25 + r, :] = bf_[at : at + 1, :]
    for q in range(4):
        piece = corner[q].astype(F32)
        for r in range(2):
            for c in range(2):
                slot = (0, 1, 4, 5)[(q % 2) * 2 + c]
                at = (6 if q < 2 else 24) + r
                colbuf[slot, at : at + 1, :] = piece[r * 2 + c : r * 2 + c + 1, :]
    for slot in range(6):
        colbuf[slot, 26:32, :] = jnp.zeros((6, width), F32)
    sub = iota((cols, width), 0)

    def spread(buf, count, r, three):
        for dx in range(3):
            for dy in range(3):
                if 0 <= r - dy < count:
                    buf[(r - dy) * cols : (r - dy + 1) * cols, (dy * 3 + dx) * width : (dy * 3 + dx + 1) * width] = three[dx]

    def shifted(row, before_col, after_col):
        left = jnp.where(sub == 0, before_col, pltpu.roll(row, 1, 0))
        right = jnp.where(sub == cols - 1, after_col, pltpu.roll(row, cols - 1, 0))
        return left.astype(BF), row.astype(BF), right.astype(BF)

    for r in range(rows + 4):
        if r < 2:
            row = top[r * cols : (r + 1) * cols, :]
        elif r < rows + 2:
            row = x_ref[(r - 2) * cols : (r - 1) * cols, :]
        else:
            row = bot[(r - rows - 2) * cols : (r - rows - 1) * cols, :]
        three = shifted(row.astype(F32), colbuf[1, 6 + r : 7 + r, :], colbuf[4, 6 + r : 7 + r, :])
        spread(im1, rows + 2, r, three)
    main = (rows + 2) * cols
    for dy in range(3):
        for dx in range(3):
            both = jnp.concatenate(
                [colbuf[dx, 6 + dy : 30 + dy, :], colbuf[3 + dx, 6 + dy : 30 + dy, :]], axis=0
            )
            im1[main : main + 48, (dy * 3 + dx) * width : (dy * 3 + dx + 1) * width] = both.astype(BF)
    loads[1].wait()
    value = dot(im1[...], w1[...]) + b1_ref[...]
    hid[...] = value / (1.0 + jnp.exp(-value))

    tall = [jnp.where(ok, 1.0, 0.0).astype(F32) for ok in (up_ok, down_ok, left_ok, right_ok)]
    for r in range(rows + 2):
        row = hid[r * cols : (r + 1) * cols, :]
        before_col = hid[main + r : main + r + 1, :] * tall[2]
        after_col = hid[main + 24 + r : main + 25 + r, :] * tall[3]
        if r in (0, rows + 1):
            f = tall[0 if r == 0 else 1]
            row, before_col, after_col = row * f, before_col * f, after_col * f
        spread(im2, rows, r, shifted(row, before_col, after_col))
    loads[2].wait()
    latent = dot(im2[...], w2[...]) + b2_ref[...]
    par[...] = dot(pick[...], latent.astype(BF)).astype(BF)
    arr[mine, :] = par[mine, :]
    send_all(par, arr, 2, cap)

    loads[3].wait()
    counts_ref[...] = dot(jnp.ones((8, slots), BF), onehot[...])[0:1, :]
    wait_all(ret, recv_sem.at[1], cap)
    chosen = dot(pick_t[...], ret[...])
    differ = latent - chosen
    grad_ref[...] = (up[...].astype(F32) + 2.0 * BETA * differ).astype(BF)
    square = differ * differ
    half = square[:, 0:LANES]
    for j in range(1, square.shape[1] // LANES):
        half = half + square[:, j * LANES : (j + 1) * LANES]
    part = jnp.sum(half.reshape(rows, cols, LANES), axis=1)
    loss_out[...] = part
    loss_in[b] = part

    def loss_copy(i):
        peer = lax.rem(b + i, cols_of)
        return pltpu.make_async_remote_copy(
            src_ref=loss_out, dst_ref=loss_in.at[b], send_sem=send_sem.at[3], recv_sem=recv_sem.at[3],
            device_id=(a, peer), device_id_type=MESH,
        )

    for i in range(1, cols_of):
        loss_copy(i).start()

    wait_all(arr, recv_sem.at[2], cap)
    others = loss_in.at[pl.ds(0, cols_of - 1)]
    pltpu.make_async_copy(others, others, recv_sem.at[3]).wait()
    total = loss_in[0]
    for i in range(1, cols_of):
        total = total + loss_in[i]
    line = jnp.sum(jnp.transpose(total), axis=0, keepdims=True)
    loss_ref[...] = BETA * line / (cols * cols_of * square.shape[1])

    pltpu.make_async_copy(others, others, send_sem.at[3]).wait()
    wait_all(req_out, send_sem.at[0], None)
    wait_all(ans, send_sem.at[1], cap)
    wait_all(par, send_sem.at[2], cap)
    for i in range(8):
        pl.when(hops[i][0])(lambda i=i: halo(i).wait_send())


def sum_body(asked, arrived, grad_in, loss_in, counts_in, grad, loss, sums, counts, hot):
    part = hot.shape[0]
    code = (iota((part, LANES), 0) + pl.program_id(0) * part + 1).astype(F32)
    for g in range(asked.shape[0]):
        same = code == asked[g, 0:1, :]
        hot[:, g * LANES : (g + 1) * LANES] = jnp.where(same, 1.0, 0.0).astype(BF)
    sums[...] = dot(hot[...], arrived[...])
    grad[...] = grad_in[...]
    loss[...] = loss_in[...]
    counts[...] = counts_in[...]


def shards(features, w_first, b_first, w_latent, b_latent, codebook, upstream, owner, local_code):
    tiles, cols_of = lax.axis_size("tile"), lax.axis_size("code")
    n = tiles * cols_of
    rows, cols, width = features.shape[3:]
    tok, latent = rows * cols, w_latent.shape[3]
    codes = codebook.shape[0]
    cap = max(16, 2 * tok // n)
    slots = n * cap
    deep = 9 * width
    vmem = pl.BlockSpec(memory_space=pltpu.VMEM)
    anyw = pl.BlockSpec(memory_space=pl.ANY)
    groups = slots // LANES
    grad, loss, counts, asked, arrived = pl.pallas_call(
        functools.partial(body, tiles, cols_of, rows, cols, cap),
        out_shape=(
            jax.ShapeDtypeStruct((tok, latent), BF),
            jax.ShapeDtypeStruct((1, rows), F32),
            jax.ShapeDtypeStruct((1, codes), F32),
            jax.ShapeDtypeStruct((groups, 8, LANES), F32),
            jax.ShapeDtypeStruct((slots, latent), BF),
        ),
        in_specs=[vmem, anyw, vmem, anyw, vmem, anyw, anyw, vmem, vmem],
        out_specs=(vmem, vmem, vmem, vmem, vmem),
        scratch_shapes=[
            pltpu.VMEM((deep, width), BF),
            pltpu.VMEM((deep, latent), BF),
            pltpu.VMEM((codes, latent), BF),
            pltpu.VMEM((tok, latent), BF),
            pltpu.VMEM((128, width), BF),
            pltpu.VMEM((2 * cols, width), BF),
            pltpu.VMEM((2 * cols, width), BF),
            pltpu.VMEM((2, 32, width), BF),
            pltpu.VMEM((4, 16, width), BF),
            pltpu.VMEM((6, 32, width), F32),
            pltpu.VMEM(((rows + 2) * cols + 48, deep), BF),
            pltpu.VMEM(((rows + 2) * cols + 48, width), F32),
            pltpu.VMEM((tok, deep), BF),
            pltpu.VMEM((n, 8, LANES), F32),
            pltpu.VMEM((n, 8, LANES), F32),
            pltpu.VMEM((slots, codes), BF),
            pltpu.VMEM((slots, tok), BF),
            pltpu.VMEM((tok, slots), BF),
            pltpu.VMEM((slots, latent), BF),
            pltpu.VMEM((slots, latent), BF),
            pltpu.VMEM((slots, latent), BF),
            pltpu.VMEM((rows, LANES), F32),
            pltpu.VMEM((cols_of, rows, LANES), F32),
            pltpu.SemaphoreType.DMA((4,)),
            pltpu.SemaphoreType.DMA((8,)),
            pltpu.SemaphoreType.DMA((8,)),
            pltpu.SemaphoreType.DMA((4,)),
            pltpu.SemaphoreType.DMA((4,)),
        ],
        compiler_params=pltpu.CompilerParams(
            collective_id=0, has_side_effects=True, vmem_limit_bytes=60 * 1024 * 1024
        ),
        name="quantize",
    )(
        features.reshape(tok, width),
        w_first.reshape(deep, width),
        b_first.reshape(1, width),
        w_latent.reshape(deep, latent),
        b_latent.reshape(1, latent),
        codebook,
        upstream.reshape(tok, latent),
        owner.reshape(1, tok),
        local_code.reshape(1, tok),
    )
    steps = 4
    part, few = codes // steps, tok // steps
    still = lambda shape: pl.BlockSpec(shape, lambda i: (0,) * len(shape))
    grad_spec = pl.BlockSpec((few, latent), lambda i: (i, 0))
    counts_spec = pl.BlockSpec((1, part), lambda i: (0, i))
    grad, loss, sums, counts = pl.pallas_call(
        sum_body,
        grid=(steps,),
        out_shape=(
            jax.ShapeDtypeStruct((tok, latent), BF),
            jax.ShapeDtypeStruct((1, rows), F32),
            jax.ShapeDtypeStruct((codes, latent), F32),
            jax.ShapeDtypeStruct((1, codes), F32),
        ),
        in_specs=[
            still((groups, 8, LANES)), still((slots, latent)), grad_spec, still((1, rows)), counts_spec,
        ],
        out_specs=(
            grad_spec, still((1, rows)), pl.BlockSpec((part, latent), lambda i: (i, 0)), counts_spec,
        ),
        scratch_shapes=[pltpu.VMEM((part, slots), BF)],
        compiler_params=pltpu.CompilerParams(vmem_limit_bytes=60 * 1024 * 1024),
        name="code_sums",
    )(asked, arrived, grad, loss, counts)
    return grad.reshape(upstream.shape), loss, sums, counts.reshape(codes)


def solution(mesh):
    in_specs = (
        P("tile", "code", None, None, None, None),
        P(),
        P(),
        P(),
        P(),
        P(("tile", "code"), None),
        P("tile", "code", None, None, None, None),
        P("tile", "code", None, None),
        P("tile", "code", None),
    )
    out_specs = (
        P("tile", "code", None, None, None, None),
        P(None, "tile"),
        P(("tile", "code"), None),
        P(("tile", "code")),
    )
    return jax.shard_map(shards, mesh=mesh, in_specs=in_specs, out_specs=out_specs, check_vma=False)
```

```python
import functools
import math

import jax
import jax.numpy as jnp
from jax import lax
from jax.experimental import pallas as pl
from jax.experimental.pallas import tpu as pltpu
from jax.sharding import PartitionSpec as P

BETA = 0.25
BF, F32, I32 = jnp.bfloat16, jnp.float32, jnp.int32
MESH = pl.DeviceIdType.MESH
LANES = 128


def iota(shape, dim):
    return lax.broadcasted_iota(I32, shape, dim)


def dot(a, b):
    return jnp.dot(a, b, preferred_element_type=F32)


def body(
    tiles, cols_of, rows, cols, cap,
    x_ref, w1_hbm, b1_ref, w2_hbm, b2_ref, book_hbm, up_hbm, own_ref, loc_ref,
    grad_ref, loss_ref, counts_ref, asked_ref, arr,
    w1, w2, book, up, pack, top, bot, side, corner, colbuf, im1, hid, im2,
    req_out, req_in, onehot, pick, pick_t, ans, ret, par, loss_out, loss_in,
    local_sem, halo_send, halo_recv, send_sem, recv_sem,
):
    n = tiles * cols_of
    tok = rows * cols
    width = x_ref.shape[1]
    codes = book.shape[0]
    slots = n * cap
    groups = slots // LANES
    per = LANES // cap
    hop = next(h for h in range(2 * n // 5, n) if math.gcd(h, n) == 1)
    a, b = lax.axis_index("tile"), lax.axis_index("code")
    me = a * cols_of + b

    loads = []
    for i, (src, dst) in enumerate(((book_hbm, book), (w1_hbm, w1), (w2_hbm, w2), (up_hbm, up))):
        copy = pltpu.make_async_copy(src, dst, local_sem.at[i])
        copy.start()
        loads.append(copy)

    def place_of(i):
        d = jnp.bitwise_xor(me, i)
        return d, (d // cols_of, lax.rem(d, cols_of))

    barrier = pltpu.get_barrier_semaphore()

    def greet(i, _):
        pl.semaphore_signal(barrier, inc=1, device_id=place_of(i)[1], device_id_type=MESH)
        return 0

    lax.fori_loop(1, n, greet, 0)

    o = iota((128, tok), 0)
    t = iota((128, tok), 1)
    col_row, col_col = o & 15, ((o >> 4) & 1) + (o >> 5) * (cols - 2)
    k, q = o & 15, (o >> 4) & 3
    cor_row = (k >> 1) + (q >> 1) * (rows - 2)
    cor_col = (k & 1) + (q & 1) * (cols - 2)
    from_col = (o < 64) & (t == col_row * cols + col_col)
    from_cor = (o >= 64) & (k < 4) & (t == cor_row * cols + cor_col)
    pack[...] = dot(jnp.where(from_col | from_cor, 1.0, 0.0).astype(BF), x_ref[...]).astype(BF)

    own = own_ref[...]
    loc = loc_ref[...]
    member = jnp.where(iota((n, tok), 0) == own, 1.0, 0.0)
    before = jnp.where(iota((tok, tok), 0) < iota((tok, tok), 1), 1.0, 0.0).astype(BF)
    earlier = dot(member.astype(BF), before)
    rank = jnp.sum(member * earlier, axis=0, keepdims=True)
    place = own.astype(F32) * cap + rank
    r8 = iota((8, tok), 0)
    stack = jnp.where(r8 == 0, rank, jnp.where(r8 == 1, loc.astype(F32), place))
    columns = jnp.transpose(stack)
    rank_c, loc_c, place_c = columns[:, 0:1], columns[:, 1:2], columns[:, 2:3]
    high = jnp.floor(loc_c * (1.0 / 64.0))
    low = loc_c - high * 64.0 + 1.0
    lane = iota((tok, LANES), 1).astype(F32)
    seat = lane == rank_c + (lax.rem(me, per) * cap).astype(F32)
    asked_high = dot(member.astype(BF), jnp.where(seat, high, 0.0).astype(BF))
    asked_low = dot(member.astype(BF), jnp.where(seat, low, 0.0).astype(BF))
    wanted = asked_high * 64.0 + asked_low
    for d in range(n):
        req_out[d] = jnp.broadcast_to(wanted[d : d + 1, :], (8, LANES))
    req_in[me] = req_out[me]

    up_ok, down_ok = a > 0, a < tiles - 1
    left_ok, right_ok = b > 0, b < cols_of - 1
    hops = (
        (up_ok, -1, 0), (down_ok, 1, 0), (left_ok, 0, -1), (right_ok, 0, 1),
        (up_ok & left_ok, -1, -1), (up_ok & right_ok, -1, 1),
        (down_ok & left_ok, 1, -1), (down_ok & right_ok, 1, 1),
    )
    edge = 2 * cols
    outgoing = (
        x_ref.at[pl.ds(0, edge)], x_ref.at[pl.ds(tok - edge, edge)],
        pack.at[pl.ds(0, 32)], pack.at[pl.ds(32, 32)],
        pack.at[pl.ds(64, 16)], pack.at[pl.ds(80, 16)],
        pack.at[pl.ds(96, 16)], pack.at[pl.ds(112, 16)],
    )
    landing = (top, bot, side.at[0], side.at[1], corner.at[0], corner.at[1], corner.at[2], corner.at[3])
    opposite = (1, 0, 3, 2, 7, 6, 5, 4)

    def halo(i):
        _, da, db = hops[i]
        return pltpu.make_async_remote_copy(
            src_ref=outgoing[i], dst_ref=landing[opposite[i]],
            send_sem=halo_send.at[i], recv_sem=halo_recv.at[opposite[i]],
            device_id=(a + da, b + db), device_id_type=MESH,
        )

    def arrival(i):
        return pltpu.make_async_copy(landing[i], landing[i], halo_recv.at[i])

    pl.semaphore_wait(barrier, n - 1)

    def send_all(src, dst, phase, rows_each):
        def step(i, _):
            d, where = place_of(i)
            if rows_each is None:
                s, r = src.at[d], dst.at[me]
            else:
                s = src.at[pl.ds(pl.multiple_of(d * rows_each, rows_each), rows_each)]
                r = dst.at[pl.ds(pl.multiple_of(me * rows_each, rows_each), rows_each)]
            pltpu.make_async_remote_copy(
                src_ref=s, dst_ref=r, send_sem=send_sem.at[phase], recv_sem=recv_sem.at[phase],
                device_id=where, device_id_type=MESH,
            ).start()
            return 0

        lax.fori_loop(1, n, step, 0)

    def wait_all(buf, sem, rows_each):
        part = buf.at[pl.ds(0, (n - 1) * (1 if rows_each is None else rows_each))]
        pltpu.make_async_copy(part, part, sem).wait()

    send_all(req_out, req_in, 0, None)
    for i in range(8):
        pl.when(hops[i][0])(lambda i=i: halo(i).start())

        @pl.when(jnp.logical_not(hops[i][0]))
        def _(i=i):
            landing[i][...] = jnp.zeros(landing[i].shape, BF)

    pick[...] = jnp.where(iota((slots, tok), 0).astype(F32) == place, 1.0, 0.0).astype(BF)
    pick_t[...] = jnp.where(iota((tok, slots), 1).astype(F32) == place_c, 1.0, 0.0).astype(BF)

    loads[0].wait()
    wait_all(req_in, recv_sem.at[0], None)
    own_group = me // per
    code_lane = iota((LANES, codes), 1).astype(F32) + 1.0

    def answer(g, _):
        group = jnp.bitwise_xor(own_group, groups - 1 - g)
        total = req_in[group * per]
        for j in range(1, per):
            total = total + req_in[group * per + j]
        asked_ref[group] = total
        here = pl.ds(pl.multiple_of(group * LANES, LANES), LANES)
        hot = jnp.where(code_lane == jnp.transpose(total)[:, 0:1], 1.0, 0.0).astype(BF)
        onehot[here, :] = hot
        ans[here, :] = dot(hot, book[...]).astype(BF)
        for j in range(per):
            d = group * per + j

            @pl.when(d != me)
            def _():
                pltpu.make_async_remote_copy(
                    src_ref=ans.at[pl.ds(pl.multiple_of(d * cap, cap), cap)],
                    dst_ref=ret.at[pl.ds(pl.multiple_of(me * cap, cap), cap)],
                    send_sem=send_sem.at[1], recv_sem=recv_sem.at[1],
                    device_id=(d // cols_of, lax.rem(d, cols_of)), device_id_type=MESH,
                ).start()
        return 0

    lax.fori_loop(0, groups, answer, 0)
    mine = pl.ds(pl.multiple_of(me * cap, cap), cap)
    ret[mine, :] = ans[mine, :]

    for i in range(8):
        pl.when(hops[i][0])(lambda i=i: arrival(i).wait())
    for s in range(2):
        for c in range(2):
            slot = (0, 1, 4, 5)[s * 2 + c]
            colbuf[slot, 8:24, :] = side[s, c * 16 : c * 16 + 16, :].astype(F32)
        slot = 2 + s
        edge_col = s * (cols - 1)
        colbuf[slot, 8:24, :] = pack[s * 48 : s * 48 + 16, :].astype(F32)
        tf, bf_ = top[...].astype(F32), bot[...].astype(F32)
        for r in range(2):
            at = r * cols + edge_col
            colbuf[slot, 6 + r : 7 + r, :] = tf[at : at + 1, :]
            colbuf[slot, 24 + r : 25 + r, :] = bf_[at : at + 1, :]
    for q in range(4):
        piece = corner[q].astype(F32)
        for r in range(2):
            for c in range(2):
                slot = (0, 1, 4, 5)[(q % 2) * 2 + c]
                at = (6 if q < 2 else 24) + r
                colbuf[slot, at : at + 1, :] = piece[r * 2 + c : r * 2 + c + 1, :]
    for slot in range(6):
        colbuf[slot, 26:32, :] = jnp.zeros((6, width), F32)
    sub = iota((cols, width), 0)

    def spread(buf, count, r, three):
        for dx in range(3):
            for dy in range(3):
                if 0 <= r - dy < count:
                    buf[(r - dy) * cols : (r - dy + 1) * cols, (dy * 3 + dx) * width : (dy * 3 + dx + 1) * width] = three[dx]

    def shifted(row, before_col, after_col):
        left = jnp.where(sub == 0, before_col, pltpu.roll(row, 1, 0))
        right = jnp.where(sub == cols - 1, after_col, pltpu.roll(row, cols - 1, 0))
        return left.astype(BF), row.astype(BF), right.astype(BF)

    for r in range(rows + 4):
        if r < 2:
            row = top[r * cols : (r + 1) * cols, :]
        elif r < rows + 2:
            row = x_ref[(r - 2) * cols : (r - 1) * cols, :]
        else:
            row = bot[(r - rows - 2) * cols : (r - rows - 1) * cols, :]
        three = shifted(row.astype(F32), colbuf[1, 6 + r : 7 + r, :], colbuf[4, 6 + r : 7 + r, :])
        spread(im1, rows + 2, r, three)
    main = (rows + 2) * cols
    for dy in range(3):
        for dx in range(3):
            both = jnp.concatenate(
                [colbuf[dx, 6 + dy : 30 + dy, :], colbuf[3 + dx, 6 + dy : 30 + dy, :]], axis=0
            )
            im1[main : main + 48, (dy * 3 + dx) * width : (dy * 3 + dx + 1) * width] = both.astype(BF)
    loads[1].wait()
    value = dot(im1[...], w1[...]) + b1_ref[...]
    hid[...] = value / (1.0 + jnp.exp(-value))

    tall = [jnp.where(ok, 1.0, 0.0).astype(F32) for ok in (up_ok, down_ok, left_ok, right_ok)]
    for r in range(rows + 2):
        row = hid[r * cols : (r + 1) * cols, :]
        before_col = hid[main + r : main + r + 1, :] * tall[2]
        after_col = hid[main + 24 + r : main + 25 + r, :] * tall[3]
        if r in (0, rows + 1):
            f = tall[0 if r == 0 else 1]
            row, before_col, after_col = row * f, before_col * f, after_col * f
        spread(im2, rows, r, shifted(row, before_col, after_col))
    loads[2].wait()
    latent = dot(im2[...], w2[...]) + b2_ref[...]
    par[...] = dot(pick[...], latent.astype(BF)).astype(BF)
    arr[mine, :] = par[mine, :]
    send_all(par, arr, 2, cap)

    loads[3].wait()
    counts_ref[...] = dot(jnp.ones((8, slots), BF), onehot[...])[0:1, :]
    wait_all(ret, recv_sem.at[1], cap)
    chosen = dot(pick_t[...], ret[...])
    differ = latent - chosen
    grad_ref[...] = (up[...].astype(F32) + 2.0 * BETA * differ).astype(BF)
    square = differ * differ
    half = square[:, 0:LANES]
    for j in range(1, square.shape[1] // LANES):
        half = half + square[:, j * LANES : (j + 1) * LANES]
    part = jnp.sum(half.reshape(rows, cols, LANES), axis=1)
    loss_out[...] = part
    loss_in[b] = part

    def loss_copy(i):
        peer = lax.rem(b + i, cols_of)
        return pltpu.make_async_remote_copy(
            src_ref=loss_out, dst_ref=loss_in.at[b], send_sem=send_sem.at[3], recv_sem=recv_sem.at[3],
            device_id=(a, peer), device_id_type=MESH,
        )

    for i in range(1, cols_of):
        loss_copy(i).start()

    wait_all(arr, recv_sem.at[2], cap)
    others = loss_in.at[pl.ds(0, cols_of - 1)]
    pltpu.make_async_copy(others, others, recv_sem.at[3]).wait()
    total = loss_in[0]
    for i in range(1, cols_of):
        total = total + loss_in[i]
    line = jnp.sum(jnp.transpose(total), axis=0, keepdims=True)
    loss_ref[...] = BETA * line / (cols * cols_of * square.shape[1])

    pltpu.make_async_copy(others, others, send_sem.at[3]).wait()
    wait_all(req_out, send_sem.at[0], None)
    wait_all(ans, send_sem.at[1], cap)
    wait_all(par, send_sem.at[2], cap)
    for i in range(8):
        pl.when(hops[i][0])(lambda i=i: halo(i).wait_send())


def sum_body(asked, arrived, grad_in, loss_in, counts_in, grad, loss, sums, counts, hot):
    part = hot.shape[0]
    code = (iota((part, LANES), 0) + pl.program_id(0) * part + 1).astype(F32)
    for g in range(asked.shape[0]):
        same = code == asked[g, 0:1, :]
        hot[:, g * LANES : (g + 1) * LANES] = jnp.where(same, 1.0, 0.0).astype(BF)
    sums[...] = dot(hot[...], arrived[...])
    grad[...] = grad_in[...]
    loss[...] = loss_in[...]
    counts[...] = counts_in[...]


def shards(features, w_first, b_first, w_latent, b_latent, codebook, upstream, owner, local_code):
    tiles, cols_of = lax.axis_size("tile"), lax.axis_size("code")
    n = tiles * cols_of
    rows, cols, width = features.shape[3:]
    tok, latent = rows * cols, w_latent.shape[3]
    codes = codebook.shape[0]
    cap = max(16, 2 * tok // n)
    slots = n * cap
    deep = 9 * width
    vmem = pl.BlockSpec(memory_space=pltpu.VMEM)
    anyw = pl.BlockSpec(memory_space=pl.ANY)
    groups = slots // LANES
    grad, loss, counts, asked, arrived = pl.pallas_call(
        functools.partial(body, tiles, cols_of, rows, cols, cap),
        out_shape=(
            jax.ShapeDtypeStruct((tok, latent), BF),
            jax.ShapeDtypeStruct((1, rows), F32),
            jax.ShapeDtypeStruct((1, codes), F32),
            jax.ShapeDtypeStruct((groups, 8, LANES), F32),
            jax.ShapeDtypeStruct((slots, latent), BF),
        ),
        in_specs=[vmem, anyw, vmem, anyw, vmem, anyw, anyw, vmem, vmem],
        out_specs=(vmem, vmem, vmem, vmem, vmem),
        scratch_shapes=[
            pltpu.VMEM((deep, width), BF),
            pltpu.VMEM((deep, latent), BF),
            pltpu.VMEM((codes, latent), BF),
            pltpu.VMEM((tok, latent), BF),
            pltpu.VMEM((128, width), BF),
            pltpu.VMEM((2 * cols, width), BF),
            pltpu.VMEM((2 * cols, width), BF),
            pltpu.VMEM((2, 32, width), BF),
            pltpu.VMEM((4, 16, width), BF),
            pltpu.VMEM((6, 32, width), F32),
            pltpu.VMEM(((rows + 2) * cols + 48, deep), BF),
            pltpu.VMEM(((rows + 2) * cols + 48, width), F32),
            pltpu.VMEM((tok, deep), BF),
            pltpu.VMEM((n, 8, LANES), F32),
            pltpu.VMEM((n, 8, LANES), F32),
            pltpu.VMEM((slots, codes), BF),
            pltpu.VMEM((slots, tok), BF),
            pltpu.VMEM((tok, slots), BF),
            pltpu.VMEM((slots, latent), BF),
            pltpu.VMEM((slots, latent), BF),
            pltpu.VMEM((slots, latent), BF),
            pltpu.VMEM((rows, LANES), F32),
            pltpu.VMEM((cols_of, rows, LANES), F32),
            pltpu.SemaphoreType.DMA((4,)),
            pltpu.SemaphoreType.DMA((8,)),
            pltpu.SemaphoreType.DMA((8,)),
            pltpu.SemaphoreType.DMA((4,)),
            pltpu.SemaphoreType.DMA((4,)),
        ],
        compiler_params=pltpu.CompilerParams(
            collective_id=0, has_side_effects=True, vmem_limit_bytes=60 * 1024 * 1024
        ),
        name="quantize",
    )(
        features.reshape(tok, width),
        w_first.reshape(deep, width),
        b_first.reshape(1, width),
        w_latent.reshape(deep, latent),
        b_latent.reshape(1, latent),
        codebook,
        upstream.reshape(tok, latent),
        owner.reshape(1, tok),
        local_code.reshape(1, tok),
    )
    steps = 2
    part, few = codes // steps, tok // steps
    still = lambda shape: pl.BlockSpec(shape, lambda i: (0,) * len(shape))
    grad_spec = pl.BlockSpec((few, latent), lambda i: (i, 0))
    counts_spec = pl.BlockSpec((1, part), lambda i: (0, i))
    grad, loss, sums, counts = pl.pallas_call(
        sum_body,
        grid=(steps,),
        out_shape=(
            jax.ShapeDtypeStruct((tok, latent), BF),
            jax.ShapeDtypeStruct((1, rows), F32),
            jax.ShapeDtypeStruct((codes, latent), F32),
            jax.ShapeDtypeStruct((1, codes), F32),
        ),
        in_specs=[
            still((groups, 8, LANES)), still((slots, latent)), grad_spec, still((1, rows)), counts_spec,
        ],
        out_specs=(
            grad_spec, still((1, rows)), pl.BlockSpec((part, latent), lambda i: (i, 0)), counts_spec,
        ),
        scratch_shapes=[pltpu.VMEM((part, slots), BF)],
        compiler_params=pltpu.CompilerParams(vmem_limit_bytes=60 * 1024 * 1024),
        name="code_sums",
    )(asked, arrived, grad, loss, counts)
    return grad.reshape(upstream.shape), loss, sums, counts.reshape(codes)


def solution(mesh):
    in_specs = (
        P("tile", "code", None, None, None, None),
        P(),
        P(),
        P(),
        P(),
        P(("tile", "code"), None),
        P("tile", "code", None, None, None, None),
        P("tile", "code", None, None),
        P("tile", "code", None),
    )
    out_specs = (
        P("tile", "code", None, None, None, None),
        P(None, "tile"),
        P(("tile", "code"), None),
        P(("tile", "code")),
    )
    return jax.shard_map(shards, mesh=mesh, in_specs=in_specs, out_specs=out_specs, check_vma=False)
```
